256 devices in a mesh: item: 8 (over z), user: 16 (over x, y), mp: 2 (over core).
Axes of the slice: x: 4, y: 4, z: 8, core: 2. Of those that a mesh axis runs over, the one named last changes fastest.
Arguments:
- item_last_hidden: bfloat16 [32768, 4096], P(('item', 'user'), 'mp'), may hold values from -6 to 6
- frozen_down_weight: bfloat16 [4096, 16], P('mp'), may hold values from -0.09375 to 0.09375
- trained_up_weight: bfloat16 [16, 4096], P(None, 'mp'), may hold values from -1.5 to 1.5
- embedding_norm_gain: float32 [4096], P('mp'), may hold values from 0.5 to 1.5
- user_context_state: bfloat16 [18432, 4096], P(('item', 'user'), 'mp'), may hold values from -110 to 110
- history_owner_device: int32 [18432, 1], P(('item', 'user')), may hold values from 0 to 127; in each aligned block of 144 rows (0 to 143, 144 to 287, ...) at most 2 rows name the same one
- history_item_row: int32 [18432], P(('item', 'user')), may hold values from 0 to 255
Outputs:
- pos_loss: float32 [18432], P(('item', 'user'))
- emb_grad: float32 [32768, 4096], P(('item', 'user'), 'mp')
- b_grad: float32 [16, 4096], P(None, 'mp')
The draws below stay inside these ranges and needn't reach their ends.
Inputs may be any that keep to these rules, and one draw needn't show every extreme that they name: `history_owner_device`: within the rows of one device no owner appears more than 2 times, and some owner appears exactly 2 times.
All inputs are finite; a program needn't handle non-finite values.
Results may differ from the reference program's by a relative error of at most 0.012.
The reference program's roundings to bfloat16 on the way (of `emb`, `hist`, `dscore` and `hist_grad`) count: a program that leaves them out, or rounds other values in their place, can miss the bound.
Values may be sent and summed in bfloat16 or wider, within the bound.
No kernel may reach another device: no remote copies, remote signals or barrier semaphores. Data moves between devices by JAX's collectives and lax.ppermute only.
A program may use at most 64 MiB of HBM per device.

```python
import math
import jax
import jax.numpy as jnp
import numpy as np
from jax import lax

MODEL_WIDTH = 4096
ADAPTER_RANK = 16
LEN = 48
ITEM_DEV = 256
HIST_DEV = 144
CAP = 2
ITEMS = 32768
TOKENS = 18432
N_ITEM = 8
N_USER = 16


def draw_user_context_state(key, part):
    key = jax.random.fold_in(key, 7)
    first = jax.random.fold_in(key, 0)
    values = jnp.clip(jax.random.normal(first, (TOKENS, MODEL_WIDTH), jnp.float32), -6.0, 6.0)
    return values.astype(jnp.bfloat16)


def set_ends(result, own_key, smallest, largest):
    dims = result.shape
    spot = [jax.random.randint(jax.random.fold_in(own_key, axis), (), 0, dims[axis]) for axis in range(len(dims))]
    result = result.at[tuple(spot)].set(smallest)
    longest = dims.index(max(dims))
    spot[longest] = (spot[longest] + 1) % dims[longest]
    return result.at[tuple(spot)].set(largest)


def steps_of(own_key, shape, shards, least, largest):
    level = 1.0
    for position, blocks in shards:
        heights = jax.random.uniform(jax.random.fold_in(jax.random.fold_in(own_key, 6), position), (blocks,), jnp.float32, least / len(shards), largest / len(shards))
        level = level * jnp.repeat(jnp.exp(heights), shape[position] // blocks).reshape((-1,) + (1,) * (len(shape) - 1 - position))
    return level


def assign_block(stream_key, own, number, rows, number_of, top, bound, slope):
    order = jax.random.permutation(stream_key, number_of)
    packed, usual = load_shares(number_of, rows * top, bound, slope, True), load_shares(number_of, rows * top, bound, slope, False)
    places = jnp.arange(number_of)

    def named(sizes, rotation):
        used = int((sizes > 0).sum())
        fixed = max(1, used // 4)
        shifted = fixed + (places - fixed + rotation * (used - fixed)) % max(1, number_of - fixed)
        return jnp.zeros((number_of,), jnp.int32).at[order[jnp.where(places < fixed, places, shifted)]].set(jnp.asarray(sizes, jnp.int32))

    sizes = jnp.where(number % 4 == 0, named(packed, number // 4), named(usual, number - number // 4 - 1))
    mixed = jax.random.permutation(jax.random.fold_in(own, 3), number_of)
    source_of, sink = mixed[0:number_of // 2 * 2:2], mixed[1:number_of // 2 * 2:2]
    margin = jnp.minimum(sizes[source_of] - 1, bound - sizes[sink]) // 2
    margin = jnp.where((source_of == order[0]) | (sink == order[0]) | (sizes[sink] == 0), 0, jnp.maximum(margin, 0))
    shifted = jax.random.randint(jax.random.fold_in(own, 4), (number_of // 2,), 0, 1 << 20) % (margin + 1)
    sizes = sizes.at[source_of].add(-shifted).at[sink].add(shifted)
    items = jnp.searchsorted(jnp.cumsum(sizes), jnp.arange(rows * top), side="right").astype(jnp.int32)
    grid = items.reshape(top, rows).T
    grid = grid[jax.random.permutation(jax.random.fold_in(own, 1), rows)]
    rotation = jax.random.randint(jax.random.fold_in(own, 2), (rows, 1), 0, top)
    return jnp.take_along_axis(grid, (jnp.arange(top)[None, :] + rotation) % top, axis=1)


def load_shares(number_of, total, reach, skew, full):
    weights = [(1 << 20) // math.isqrt(grade ** skew) + 1 for grade in range(1, number_of + 1)]
    largest = reach if full else min(reach, max(-(-total // number_of), total * weights[0] // sum(weights)))
    least = 1 if total - largest >= number_of - 1 else 0
    counts, rest = [largest] + [least] * (number_of - 1), total - largest - least * (number_of - 1)
    while rest > 0:
        candidates = [i for i in range(1, number_of) if counts[i] < largest] or [i for i in range(1, number_of) if counts[i] < reach]
        whole, remaining = sum([weights[i] for i in candidates]), rest
        for i in candidates:
            more = min(reach - counts[i], max(1, remaining * weights[i] // whole), rest)
            counts[i] = counts[i] + more
            rest = rest - more
    return np.array(counts)


def gaussian(stream_key, shape, deviation, reach, cuts=(), kind=jnp.bfloat16):
    array = jax.random.normal(stream_key, shape, jnp.float32) * deviation
    if len(cuts) > 0:
        array = steps_of(stream_key, shape, cuts, -0.22, 0.18) * array
    return jnp.clip(array, min=-reach, max=reach).astype(kind)


def setup_inputs(seed: int = 0) -> dict:
    seeds = jax.random.split(jax.random.key(seed), 8)
    item_last_hidden = gaussian(seeds[0], (ITEMS, MODEL_WIDTH), 1.0, 6.0, ((0, 128), (1, 2)))
    frozen_down_weight = gaussian(seeds[1], (MODEL_WIDTH, ADAPTER_RANK), MODEL_WIDTH ** -0.5, 0.09375, ((0, 2),))
    trained_up_weight = gaussian(seeds[2], (ADAPTER_RANK, MODEL_WIDTH), ADAPTER_RANK ** -0.5, 1.5, ((1, 2),))
    embedding_norm_gain = jnp.clip(1.0 + 0.1 * jax.random.normal(seeds[3], (MODEL_WIDTH,), jnp.float32), 0.5, 1.5)
    user_context_state = draw_user_context_state(jax.random.fold_in(seeds[7], 71), 0)
    history_owner_device_keys = jax.random.split(jax.random.fold_in(seeds[5], 1), TOKENS // HIST_DEV)
    history_owner_device_turns = jax.random.permutation(jax.random.fold_in(seeds[5], 3), TOKENS // HIST_DEV)
    history_owner_device = jax.vmap(lambda own, number: assign_block(jax.random.fold_in(seeds[5], 2), own, number, HIST_DEV, N_ITEM * N_USER, 1, CAP, 2))(history_owner_device_keys, history_owner_device_turns).reshape((TOKENS, 1))
    history_item_row = set_ends(jax.random.randint(seeds[6], (TOKENS,), 0, ITEM_DEV), jax.random.fold_in(seeds[6], 1), 0, ITEM_DEV - 1).astype(jnp.int32)
    return dict(item_last_hidden=item_last_hidden, frozen_down_weight=frozen_down_weight, trained_up_weight=trained_up_weight, embedding_norm_gain=embedding_norm_gain, user_context_state=user_context_state, history_owner_device=history_owner_device, history_item_row=history_item_row)


EPS = 1e-06

def group_step(cands, queries):
    width = cands.shape[0]
    scores = jnp.dot(queries, cands.T, preferred_element_type=jnp.float32) / math.sqrt(MODEL_WIDTH)
    top = lax.optimization_barrier(jnp.max(scores, axis=1, keepdims=True))
    lse = top + jnp.log(lax.optimization_barrier(jnp.sum(jnp.exp(scores - top), axis=1, keepdims=True)))
    index = jnp.arange(width, dtype=jnp.int32)
    target = jnp.minimum(index + 1, width - 1).astype(jnp.int32)
    valid = index % LEN != LEN - 1
    positive = jnp.take_along_axis(scores, target[:, None], axis=1)
    loss = jnp.where(valid, (lse - positive)[:, 0], jnp.float32(0.0))
    hit = (index[None, :] == target[:, None]).astype(jnp.float32)
    dscore = jnp.where(valid[:, None], jnp.exp(scores - lse) - hit, jnp.float32(0.0)).astype(jnp.bfloat16)
    blocks = dscore.reshape(N_USER, HIST_DEV, width)
    query_blocks = queries.reshape(N_USER, HIST_DEV, MODEL_WIDTH)

    def add_block(total, pair):
        term = jnp.dot(pair[0].T, pair[1], preferred_element_type=jnp.float32).astype(jnp.bfloat16)
        term = lax.optimization_barrier(term)
        return (total + term.astype(jnp.float32), None)
    grad, _ = lax.scan(add_block, jnp.zeros((width, MODEL_WIDTH), jnp.float32), (blocks, query_blocks))
    return (loss, grad.astype(jnp.bfloat16))

def reference(item_last_hidden, frozen_down_weight, trained_up_weight, embedding_norm_gain, user_context_state, history_owner_device, history_item_row):
    low_rank_output = jnp.dot(item_last_hidden, frozen_down_weight, preferred_element_type=jnp.float32)
    pre_norm_input = item_last_hidden.astype(jnp.float32) + jnp.dot(low_rank_output, trained_up_weight.astype(jnp.float32), precision=lax.Precision.HIGHEST)
    rinv = lax.rsqrt(lax.optimization_barrier(jnp.mean(pre_norm_input * pre_norm_input, axis=1, keepdims=True)) + EPS)
    emb = (pre_norm_input * rinv * embedding_norm_gain).astype(jnp.bfloat16)
    flat = (history_owner_device[:, 0] * ITEM_DEV + history_item_row).astype(jnp.int32)
    hist = emb[flat]
    width = N_USER * HIST_DEV
    cands = hist.reshape(N_ITEM, width, MODEL_WIDTH)
    queries = user_context_state.reshape(N_ITEM, width, MODEL_WIDTH)
    losses, grads = lax.map(lambda pair: group_step(pair[0], pair[1]), (cands, queries))
    pos_loss = losses.reshape(-1)
    hist_grad = grads.reshape(-1, MODEL_WIDTH)
    emb_grad = jax.ops.segment_sum(hist_grad.astype(jnp.float32), flat, num_segments=ITEM_DEV * N_ITEM * N_USER)
    scaled = emb_grad * embedding_norm_gain
    inner = lax.optimization_barrier(jnp.mean(pre_norm_input * scaled, axis=1, keepdims=True))
    dpre = rinv * scaled - pre_norm_input * rinv * rinv * rinv * inner
    b_grad = jnp.dot(low_rank_output.T, dpre, precision=lax.Precision.HIGHEST)
    return (pos_loss, emb_grad, b_grad)
```

```python
import math

import jax
import jax.numpy as jnp
from jax import lax
from jax.sharding import PartitionSpec as P

MODEL_WIDTH = 4096
LEN = 48
EPS = 1e-06
LOWEST = -1e30


def exchange(x, axis):
    return lax.all_to_all(x, axis, split_axis=0, concat_axis=0, tiled=True)


def swap(x):
    return lax.ppermute(x, "mp", [(0, 1), (1, 0)])


def plane_shift(x, step):
    planes = lax.axis_size("item")
    return lax.ppermute(x, "item", [(z, (z + step) % planes) for z in range(planes)])


def body(
    item_last_hidden,
    frozen_down_weight,
    trained_up_weight,
    embedding_norm_gain,
    user_context_state,
    history_owner_device,
    history_item_row,
):
    stored, part_width = item_last_hidden.shape
    count = history_item_row.shape[0]
    planes = lax.axis_size("item")
    users = lax.axis_size("user")
    devices = planes * users
    group = users * count
    slots = 2 * users
    total = planes * slots
    z = lax.axis_index("item")
    me = lax.axis_index("user")

    queries = lax.all_gather(user_context_state, "user", axis=0, tiled=True)

    code = jnp.arange(count, dtype=jnp.int32) * stored + history_item_row
    named = history_owner_device == jnp.arange(devices, dtype=jnp.int32)[None, :]
    first = jnp.min(jnp.where(named, code[:, None], count * stored), axis=0)
    last = jnp.max(jnp.where(named, code[:, None], -1), axis=0)
    wanted = jnp.stack([jnp.where(last < 0, -1, first), jnp.where(last > first, last, -1)], axis=1)
    asked = exchange(wanted, ("item", "user")).reshape(planes, slots)
    asked = lax.dynamic_slice_in_dim(jnp.concatenate([asked, asked]), z, planes, 0).reshape(total)
    asked_row = jnp.where(asked < 0, -1, asked % stored)
    asked_place = jnp.where(asked < 0, -1, asked // stored)

    rows = item_last_hidden[jnp.maximum(asked_row, 0)]
    note = jnp.broadcast_to(asked_place.astype(jnp.bfloat16)[:, None], (total, 128))
    packet = jnp.concatenate([rows, note], axis=1).reshape(planes, slots, part_width + 128)
    arrived = jnp.concatenate(
        [packet[0]] + [plane_shift(packet[d], d) for d in range(1, planes)], axis=0
    )
    hidden = arrived[:, :part_width]
    place = arrived[:, part_width].astype(jnp.int32)
    asker = (jnp.arange(total, dtype=jnp.int32) % slots) // 2
    used = place >= 0
    position = jnp.where(used, asker * count + place, -1)

    low = jnp.dot(hidden, frozen_down_weight, preferred_element_type=jnp.float32)
    low = low + swap(low)
    pre = hidden.astype(jnp.float32) + jnp.dot(
        low, trained_up_weight.astype(jnp.float32), precision=lax.Precision.HIGHEST
    )
    squares = jnp.sum(pre * pre, axis=1, keepdims=True)
    squares = squares + swap(squares)
    rinv = lax.rsqrt(squares / MODEL_WIDTH + EPS)
    hist = (pre * rinv * embedding_norm_gain).astype(jnp.bfloat16)

    partial = lax.dot_general(
        queries, hist, (((1,), (1,)), ((), ())), preferred_element_type=jnp.float32
    )
    scores = (partial + swap(partial)) / math.sqrt(MODEL_WIDTH)
    line = jnp.arange(group, dtype=jnp.int32)
    valid = line % LEN != LEN - 1
    hit = (line[:, None] + 1 == position[None, :]) & valid[:, None]
    scores = jnp.where(used[None, :], scores, LOWEST)
    top = jnp.max(scores, axis=1)
    mass = jnp.sum(jnp.where(used[None, :], jnp.exp(scores - top[:, None]), 0.0), axis=1)
    positive = jnp.sum(jnp.where(hit, scores, 0.0), axis=1)
    stats = jnp.stack([top, mass, positive])
    stats = exchange(jnp.broadcast_to(stats[None], (users, 3, group)), "user")
    peak = jnp.max(stats[:, 0], axis=0)
    lse = peak + jnp.log(jnp.sum(stats[:, 1] * jnp.exp(stats[:, 0] - peak[None]), axis=0))
    loss = jnp.where(valid, lse - jnp.sum(stats[:, 2], axis=0), 0.0)
    pos_loss = lax.dynamic_slice_in_dim(loss, me * count, count, 0)

    dscore = jnp.where(used[None, :], jnp.exp(scores - lse[:, None]), 0.0) - hit.astype(jnp.float32)
    dscore = jnp.where(valid[:, None], dscore, 0.0).astype(jnp.bfloat16)
    hist_grad = lax.dot_general(
        dscore, queries, (((0,), (0,)), ((), ())), preferred_element_type=jnp.float32
    ).astype(jnp.bfloat16)

    outgoing = hist_grad.reshape(planes, slots, part_width)
    returned = jnp.concatenate(
        [outgoing[0]] + [plane_shift(outgoing[d], -d) for d in range(1, planes)], axis=0
    )
    picker = (jnp.arange(stored, dtype=jnp.int32)[:, None] == asked_row[None, :]).astype(
        jnp.bfloat16
    )
    emb_grad = jnp.dot(picker, returned, preferred_element_type=jnp.float32)

    scaled = hist_grad.astype(jnp.float32) * embedding_norm_gain
    inner = jnp.sum(pre * scaled, axis=1, keepdims=True)
    inner = (inner + swap(inner)) / MODEL_WIDTH
    dpre = rinv * scaled - pre * rinv * rinv * rinv * inner
    b_part = jnp.dot(low.T, dpre, precision=lax.Precision.HIGHEST)
    rank = b_part.shape[0]
    share = part_width // users
    b_part = b_part.reshape(rank, users, share).transpose(1, 0, 2)
    b_part = jnp.sum(exchange(b_part, "user"), axis=0)
    b_part = jnp.sum(
        exchange(jnp.broadcast_to(b_part[None], (planes, rank, share)), "item"), axis=0
    )
    b_grad = exchange(jnp.broadcast_to(b_part[None], (users, rank, share)), "user")
    b_grad = b_grad.transpose(1, 0, 2).reshape(rank, part_width)
    return (pos_loss, emb_grad, b_grad)


def solution(mesh):
    placed = (
        P(("item", "user"), "mp"),
        P("mp", None),
        P(None, "mp"),
        P("mp"),
        P(("item", "user"), "mp"),
        P(("item", "user"), None),
        P(("item", "user")),
    )
    return jax.shard_map(
        body,
        mesh=mesh,
        in_specs=placed,
        out_specs=(P(("item", "user")), P(("item", "user"), "mp"), P(None, "mp")),
        check_vma=False,
    )
```

```python
import functools
import math

import jax
import jax.numpy as jnp
from jax import lax
from jax.experimental import pallas as pl
from jax.experimental.pallas import tpu as pltpu
from jax.sharding import PartitionSpec as P

MODEL_WIDTH = 4096
LEN = 48
EPS = 1e-06
LOWEST = -1e30
MIB = 1024 * 1024


def exchange(x, axis):
    return lax.all_to_all(x, axis, split_axis=0, concat_axis=0, tiled=True)


def swap(x):
    return lax.ppermute(x, "mp", [(0, 1), (1, 0)])


def plane_shift(x, step):
    planes = lax.axis_size("item")
    return lax.ppermute(x, "item", [(z, (z + step) % planes) for z in range(planes)])


def plane_pair(x, mask):
    planes = lax.axis_size("item")
    return lax.ppermute(x, "item", [(z, z ^ mask) for z in range(planes)])


def from_x(x, step):
    side = math.isqrt(lax.axis_size("user"))
    pairs = [(((u // side + step) % side) * side + u % side, u) for u in range(side * side)]
    return lax.ppermute(x, "user", pairs)


def from_y(x, step):
    side = math.isqrt(lax.axis_size("user"))
    pairs = [((u // side) * side + (u % side + step) % side, u) for u in range(side * side)]
    return lax.ppermute(x, "user", pairs)


def ring(block, first, second, at):
    rows, width = block.shape
    cut = rows // 2 // 8 * 8
    near = first(block, 1)
    back = first(block, -1)
    far_top = first(near[:cut], 1)
    far_low = first(back[cut:], -1)
    line = jnp.zeros((4 * rows, width), block.dtype)
    for step, piece, start in ((0, block, 0), (1, near, 0), (3, back, 0), (2, far_top, 0), (2, far_low, cut)):
        line = lax.dynamic_update_slice(line, piece, ((at + step) % 4 * rows + start, 0))
    up = second(line, 1)
    down = second(line, -1)
    half = 2 * rows
    up_two = second(up[:half], 1)
    down_two = second(down[half:], -1)
    return line, up, down, up_two, down_two


def line_places(at, rows):
    whole = 4 * rows
    return (
        (at * whole, whole),
        ((at + 1) % 4 * whole, whole),
        ((at + 3) % 4 * whole, whole),
        ((at + 2) % 4 * whole, whole // 2),
        ((at + 2) % 4 * whole + whole // 2, whole // 2),
    )


def scores_kernel(rows, at_ref, hist_ref, *refs):
    pieces, out_ref, held, sems = refs[:5], refs[5], refs[6], refs[7]
    places = line_places(at_ref[0], rows)
    copies = []
    for i, (start, size) in enumerate(places):
        spot = pl.ds(pl.multiple_of(start, 16), size)
        copies.append(pltpu.make_async_copy(pieces[i], held.at[spot], sems.at[i]))
        copies[-1].start()
    for i, (start, size) in enumerate(places):
        copies[i].wait()
        spot = pl.ds(pl.multiple_of(start, 16), size)
        out_ref[spot, :] = lax.dot_general(
            held[spot, :],
            hist_ref[...],
            (((1,), (1,)), ((), ())),
            preferred_element_type=jnp.float32,
        )


def partial_scores(at, hist, pieces, rows):
    total, width = hist.shape
    lines = 16 * rows
    vmem = pl.BlockSpec(memory_space=pltpu.VMEM)
    return pl.pallas_call(
        functools.partial(scores_kernel, rows),
        out_shape=jax.ShapeDtypeStruct((lines, total), jnp.float32),
        in_specs=[pl.BlockSpec(memory_space=pltpu.SMEM), vmem]
        + [pl.BlockSpec(memory_space=pl.ANY)] * 5,
        out_specs=vmem,
        scratch_shapes=[pltpu.VMEM((lines, width), jnp.bfloat16), pltpu.SemaphoreType.DMA((5,))],
        compiler_params=pltpu.CompilerParams(vmem_limit_bytes=16 * MIB),
        cost_estimate=pl.CostEstimate(
            flops=2 * lines * total * width, bytes_accessed=2 * lines * width, transcendentals=0
        ),
    )(at, hist, *pieces)


def grad_kernel(rows, planes, at_ref, left_ref, right_ref, *refs):
    pieces, outs = refs[:10], refs[10 : 10 + planes]
    held, sems = refs[10 + planes], refs[11 + planes]
    lines = 16 * rows
    copies = []
    for side in range(2):
        for i, (start, size) in enumerate(line_places(at_ref[side], rows)):
            spot = pl.ds(pl.multiple_of(side * lines + start, 16), size)
            number = 5 * side + i
            copies.append(
                pltpu.make_async_copy(pieces[number], held.at[spot], sems.at[number])
            )
            copies[-1].start()
    width = held.shape[1]
    tile = 512
    slots = outs[0].shape[0]
    for copy in copies:
        copy.wait()
    for start in range(0, width, tile):
        spot = slice(start, start + tile)
        dims = (((0,), (0,)), ((), ()))
        grad = lax.dot_general(
            left_ref[...], held[:lines, spot], dims, preferred_element_type=jnp.float32
        ) + lax.dot_general(
            right_ref[...], held[lines:, spot], dims, preferred_element_type=jnp.float32
        )
        grad = grad.astype(jnp.bfloat16)
        for d in range(planes):
            outs[d][:, spot] = grad[d * slots : (d + 1) * slots]


def history_gradient(at, left, right, pieces, rows, planes):
    lines, total = left.shape
    width = pieces[0].shape[1]
    vmem = pl.BlockSpec(memory_space=pltpu.VMEM)
    return pl.pallas_call(
        functools.partial(grad_kernel, rows, planes),
        out_shape=[jax.ShapeDtypeStruct((total // planes, width), jnp.bfloat16)] * planes,
        in_specs=[pl.BlockSpec(memory_space=pltpu.SMEM), vmem, vmem]
        + [pl.BlockSpec(memory_space=pl.ANY)] * 10,
        out_specs=[vmem] * planes,
        scratch_shapes=[
            pltpu.VMEM((2 * lines, width), jnp.bfloat16),
            pltpu.SemaphoreType.DMA((10,)),
        ],
        compiler_params=pltpu.CompilerParams(vmem_limit_bytes=28 * MIB),
        cost_estimate=pl.CostEstimate(
            flops=4 * lines * total * width, bytes_accessed=4 * lines * width, transcendentals=0
        ),
    )(at, left, right, *pieces)


def pick_kernel(row_ref, *refs):
    pieces, out_ref = refs[:-1], refs[-1]
    stored = out_ref.shape[0]
    total = row_ref.shape[1]
    item = lax.broadcasted_iota(jnp.int32, (stored, total), 0)
    picker = jnp.where(item == row_ref[...], 1.0, 0.0).astype(jnp.bfloat16)
    grads = jnp.concatenate([piece[...] for piece in pieces], axis=0)
    out_ref[...] = jnp.dot(picker, grads, preferred_element_type=jnp.float32)


def sum_by_item(row, pieces, stored):
    slots, width = pieces[0].shape
    tile = 512
    total = row.shape[0]
    return pl.pallas_call(
        pick_kernel,
        grid=(width // tile,),
        out_shape=jax.ShapeDtypeStruct((stored, width), jnp.float32),
        in_specs=[pl.BlockSpec((1, total), lambda j: (0, 0))]
        + [pl.BlockSpec((slots, tile), lambda j: (0, j))] * len(pieces),
        out_specs=pl.BlockSpec((stored, tile), lambda j: (0, j)),
        cost_estimate=pl.CostEstimate(
            flops=2 * stored * total * width, bytes_accessed=6 * total * width, transcendentals=0
        ),
    )(row[None], *pieces)


def body(
    item_last_hidden,
    frozen_down_weight,
    trained_up_weight,
    embedding_norm_gain,
    user_context_state,
    history_owner_device,
    history_item_row,
):
    stored, part_width = item_last_hidden.shape
    count = history_item_row.shape[0]
    planes = lax.axis_size("item")
    users = lax.axis_size("user")
    devices = planes * users
    slots = 2 * users
    total = planes * slots
    half = count // 2
    z = lax.axis_index("item")
    me = lax.axis_index("user")
    my_x, my_y = me // 4, me % 4

    left = ring(user_context_state[:half], from_x, from_y, my_x)
    right = ring(user_context_state[half:], from_y, from_x, my_y)

    code = jnp.arange(count, dtype=jnp.int32) * stored + history_item_row
    named = history_owner_device == jnp.arange(devices, dtype=jnp.int32)[None, :]
    first = jnp.min(jnp.where(named, code[:, None], count * stored), axis=0)
    last = jnp.max(jnp.where(named, code[:, None], -1), axis=0)
    wanted = jnp.stack([jnp.where(last < 0, -1, first), jnp.where(last > first, last, -1)], axis=1)
    asked = exchange(wanted, ("item", "user")).reshape(planes, slots)
    asked = lax.dynamic_slice_in_dim(jnp.concatenate([asked, asked]), z, planes, 0).reshape(total)
    asked_row = jnp.where(asked < 0, -1, asked % stored)
    asked_place = jnp.where(asked < 0, -1, asked // stored)

    rows = item_last_hidden[jnp.maximum(asked_row, 0)]
    note = jnp.broadcast_to(asked_place.astype(jnp.bfloat16)[:, None], (total, 128))
    packet = jnp.concatenate([rows, note], axis=1).reshape(planes, slots, part_width + 128)
    arrived = jnp.concatenate(
        [packet[0]] + [plane_shift(packet[d], d) for d in range(1, planes)], axis=0
    )
    hidden = arrived[:, :part_width]
    place = arrived[:, part_width].astype(jnp.int32)
    asker = (jnp.arange(total, dtype=jnp.int32) % slots) // 2
    used = place >= 0
    position = jnp.where(used, asker * count + place, -1)

    low = jnp.dot(hidden, frozen_down_weight, preferred_element_type=jnp.float32)
    low = low + swap(low)
    pre = hidden.astype(jnp.float32) + jnp.dot(
        low, trained_up_weight.astype(jnp.float32), precision=lax.Precision.HIGHEST
    )
    squares = jnp.sum(pre * pre, axis=1, keepdims=True)
    squares = squares + swap(squares)
    rinv = lax.rsqrt(squares / MODEL_WIDTH + EPS)
    hist = (pre * rinv * embedding_norm_gain).astype(jnp.bfloat16)

    at_left, at_right = my_y.astype(jnp.int32), my_x.astype(jnp.int32)
    places = jnp.arange(users, dtype=jnp.int32)[:, None]
    inside = jnp.arange(half, dtype=jnp.int32)[None, :]
    sides = []
    for pieces, at, owner, shift in (
        (left, at_left, places % 4 * 4 + places // 4, 0),
        (right, at_right, places, half),
    ):
        partial = partial_scores(at.reshape(1), hist, pieces, half)
        line = (owner * count + inside + shift).reshape(-1)
        sides.append((partial, swap(partial), line))
    scores, stats = [], []
    for partial, other, line in sides:
        valid = line % LEN != LEN - 1
        hit = (line[:, None] + 1 == position[None, :]) & valid[:, None]
        score = jnp.where(used[None, :], (partial + other) / math.sqrt(MODEL_WIDTH), LOWEST)
        top = jnp.max(score, axis=1)
        mass = jnp.sum(jnp.where(used[None, :], jnp.exp(score - top[:, None]), 0.0), axis=1)
        positive = jnp.sum(jnp.where(hit, score, 0.0), axis=1)
        scores.append((score, hit, valid))
        stats.append((top, mass, positive))
    tops, masses, positives = [jnp.stack(s) for s in zip(*stats)]
    sent = jnp.stack([tops, masses])
    sent = exchange(jnp.broadcast_to(sent[None], (users,) + sent.shape), "user")
    peak = jnp.max(sent[:, 0], axis=0)
    lse = peak + jnp.log(jnp.sum(sent[:, 1] * jnp.exp(sent[:, 0] - peak[None]), axis=0))

    dscores = []
    for side, (score, hit, valid) in enumerate(scores):
        dscore = jnp.where(used[None, :], jnp.exp(score - lse[side][:, None]), 0.0)
        dscore = dscore - hit.astype(jnp.float32)
        dscores.append(jnp.where(valid[:, None], dscore, 0.0).astype(jnp.bfloat16))
    outgoing = history_gradient(
        jnp.stack([at_left, at_right]), dscores[0], dscores[1], left + right, half, planes
    )
    returned = [outgoing[0]] + [plane_shift(outgoing[d], -d) for d in range(1, planes)]
    emb_grad = sum_by_item(asked_row, returned, stored)

    scaled = jnp.concatenate(outgoing, axis=0).astype(jnp.float32) * embedding_norm_gain
    inner = jnp.sum(pre * scaled, axis=1, keepdims=True)
    inner = (inner + swap(inner)) / MODEL_WIDTH
    dpre = rinv * scaled - pre * rinv * rinv * rinv * inner
    b_part = jnp.dot(low.T, dpre, precision=lax.Precision.HIGHEST)
    rank = b_part.shape[0]
    share = part_width // users
    b_part = b_part.reshape(rank, users, share).transpose(1, 0, 2)
    positives = positives.reshape(2, 4, 4, half)
    positives = jnp.stack([positives[0].transpose(1, 0, 2), positives[1]], axis=2)
    positives = positives.reshape(users, 2, half)
    positives = jnp.pad(positives, ((0, 0), (0, 0), (0, share - half)))
    summed = jnp.sum(exchange(jnp.concatenate([b_part, positives], axis=1), "user"), axis=0)
    positive = summed[rank:, :half].reshape(count)
    own = jnp.concatenate(
        [
            lax.dynamic_slice_in_dim(lse[0], (my_y * 4 + my_x) * half, half, 0),
            lax.dynamic_slice_in_dim(lse[1], (my_x * 4 + my_y) * half, half, 0),
        ]
    )
    inside = jnp.arange(count, dtype=jnp.int32)
    pos_loss = jnp.where(inside % LEN != LEN - 1, own - positive, 0.0)

    b_part = summed[:rank]
    for mask in (1, 2, 4):
        b_part = b_part + plane_pair(b_part, mask)
    b_grad = exchange(jnp.broadcast_to(b_part[None], (users, rank, share)), "user")
    b_grad = b_grad.transpose(1, 0, 2).reshape(rank, part_width)
    return (pos_loss, emb_grad, b_grad)


def solution(mesh):
    placed = (
        P(("item", "user"), "mp"),
        P("mp", None),
        P(None, "mp"),
        P("mp"),
        P(("item", "user"), "mp"),
        P(("item", "user"), None),
        P(("item", "user")),
    )
    return jax.shard_map(
        body,
        mesh=mesh,
        in_specs=placed,
        out_specs=(P(("item", "user")), P(("item", "user"), "mp"), P(None, "mp")),
        check_vma=False,
    )
```

```python
import math

import jax
import jax.numpy as jnp
from jax import lax
from jax.experimental import pallas as pl
from jax.experimental.pallas import tpu as pltpu
from jax.sharding import PartitionSpec as P

MODEL_WIDTH = 4096
LEN = 48
EPS = 1e-06
LOWEST = -1e30
MIB = 1024 * 1024


def exchange(x, axis):
    return lax.all_to_all(x, axis, split_axis=0, concat_axis=0, tiled=True)


def swap(x):
    return lax.ppermute(x, "mp", [(0, 1), (1, 0)])


def turn(x, by):
    return lax.dynamic_slice_in_dim(jnp.concatenate([x, x[:3]]), by, 4, 0)


def from_x(x, step):
    pairs = [((u // 4 + step) % 4 * 4 + u % 4, u) for u in range(16)]
    return lax.ppermute(x, "user", pairs)


def from_y(x, step):
    pairs = [(u // 4 * 4 + (u % 4 + step) % 4, u) for u in range(16)]
    return lax.ppermute(x, "user", pairs)


def add_kernel(left_ref, right_ref, *refs):
    refs[-1][...] = left_ref[...] + right_ref[...]


def add_after(left, right, pieces):
    vmem = pl.BlockSpec(memory_space=pltpu.VMEM)
    return pl.pallas_call(
        add_kernel,
        out_shape=jax.ShapeDtypeStruct(left.shape, left.dtype),
        in_specs=[vmem, vmem] + [pl.BlockSpec(memory_space=pl.ANY)] * len(pieces),
        out_specs=vmem,
        compiler_params=pltpu.CompilerParams(vmem_limit_bytes=4 * MIB),
        cost_estimate=pl.CostEstimate(
            flops=left.size, bytes_accessed=12 * left.size, transcendentals=0
        ),
    )(left, right, *pieces)


def plane_pair(x, mask):
    planes = lax.axis_size("item")
    return lax.ppermute(x, "item", [(z, z ^ mask) for z in range(planes)])


def body(
    item_last_hidden,
    frozen_down_weight,
    trained_up_weight,
    embedding_norm_gain,
    user_context_state,
    history_owner_device,
    history_item_row,
):
    stored, part_width = item_last_hidden.shape
    count = history_item_row.shape[0]
    planes = lax.axis_size("item")
    users = lax.axis_size("user")
    devices = planes * users
    group = users * count
    slots = 2 * users
    total = planes * slots
    me = lax.axis_index("user")

    queries = lax.all_gather(user_context_state, "user", axis=0, tiled=True)

    code = jnp.arange(count, dtype=jnp.int32) * stored + history_item_row
    named = history_owner_device == jnp.arange(devices, dtype=jnp.int32)[None, :]
    first = jnp.min(jnp.where(named, code[:, None], count * stored), axis=0)
    last = jnp.max(jnp.where(named, code[:, None], -1), axis=0)
    wanted = jnp.stack([jnp.where(last < 0, -1, first), jnp.where(last > first, last, -1)], axis=1)
    asked = exchange(wanted, ("item", "user")).reshape(planes, slots)
    asked = asked.reshape(total)
    asked_row = jnp.where(asked < 0, -1, asked % stored)
    asked_place = jnp.where(asked < 0, -1, asked // stored)

    rows = item_last_hidden[jnp.maximum(asked_row, 0)]
    note = jnp.broadcast_to(asked_place.astype(jnp.bfloat16)[:, None], (total, 128))
    packet = jnp.concatenate([rows, note], axis=1).reshape(planes, slots, part_width + 128)
    arrived = exchange(packet, "item").reshape(total, part_width + 128)
    hidden = arrived[:, :part_width]
    place = arrived[:, part_width].astype(jnp.int32)
    asker = (jnp.arange(total, dtype=jnp.int32) % slots) // 2
    used = place >= 0
    position = jnp.where(used, asker * count + place, -1)

    low = jnp.dot(hidden, frozen_down_weight, preferred_element_type=jnp.float32)
    low = low + swap(low)
    pre = hidden.astype(jnp.float32) + jnp.dot(
        low, trained_up_weight.astype(jnp.float32), precision=lax.Precision.HIGHEST
    )
    squares = jnp.sum(pre * pre, axis=1, keepdims=True)
    squares = squares + swap(squares)
    rinv = lax.rsqrt(squares / MODEL_WIDTH + EPS)
    hist = (pre * rinv * embedding_norm_gain).astype(jnp.bfloat16)

    line = jnp.arange(group, dtype=jnp.int32)
    valid = line % LEN != LEN - 1
    hit = (line[:, None] + 1 == position[None, :]) & valid[:, None]
    cut = group // 2
    hist = lax.optimization_barrier(hist)
    partials = [
        lax.dot_general(
            part, hist, (((1,), (1,)), ((), ())), preferred_element_type=jnp.float32
        )
        for part in (queries[:cut], queries[cut:])
    ]
    sums = jnp.concatenate([partial + swap(partial) for partial in partials], axis=0)
    scores = jnp.where(used[None, :], sums / math.sqrt(MODEL_WIDTH), LOWEST)
    top = jnp.max(scores, axis=1)
    mass = jnp.sum(jnp.where(used[None, :], jnp.exp(scores - top[:, None]), 0.0), axis=1)
    positive = jnp.sum(jnp.where(hit, scores, 0.0), axis=1)
    stats = jnp.stack([top, mass])
    stats = exchange(jnp.broadcast_to(stats[None], (users, 2, group)), "user")
    peak = jnp.max(stats[:, 0], axis=0)
    lse = peak + jnp.log(jnp.sum(stats[:, 1] * jnp.exp(stats[:, 0] - peak[None]), axis=0))

    dscore = jnp.where(used[None, :], jnp.exp(scores - lse[:, None]), 0.0) - hit.astype(jnp.float32)
    dscore = jnp.where(valid[:, None], dscore, 0.0).astype(jnp.bfloat16)
    dscore = lax.optimization_barrier(dscore)
    hist_grad = lax.dot_general(
        dscore, queries, (((0,), (0,)), ((), ())), preferred_element_type=jnp.float32
    ).astype(jnp.bfloat16)
    hist_grad = lax.optimization_barrier(hist_grad)

    outgoing = hist_grad.reshape(planes, slots, part_width)
    returned = exchange(outgoing, "item").reshape(total, part_width)
    picker = (jnp.arange(stored, dtype=jnp.int32)[:, None] == asked_row[None, :]).astype(
        jnp.bfloat16
    )
    emb_grad = jnp.dot(picker, returned, preferred_element_type=jnp.float32)

    scaled = hist_grad.astype(jnp.float32) * embedding_norm_gain
    inner = jnp.sum(pre * scaled, axis=1, keepdims=True)
    inner = (inner + swap(inner)) / MODEL_WIDTH
    dpre = rinv * scaled - pre * rinv * rinv * rinv * inner
    b_part = jnp.dot(low.T, dpre, precision=lax.Precision.HIGHEST)
    rank = b_part.shape[0]
    share = part_width // users
    b_part = b_part.reshape(rank, users, share).transpose(1, 0, 2)
    positive = jnp.pad(positive.reshape(users, 2, count // 2), ((0, 0), (0, 0), (0, share - count // 2)))
    both = jnp.concatenate([b_part, positive], axis=1).reshape(4, 4, rank + 2, share)
    both = turn(both, me // 4)
    both = both[0] + from_x(both[3], 1) + from_x(both[2], 2) + from_x(both[1], 3)
    both = turn(both, me % 4)
    summed = both[0] + from_y(both[3], 1) + from_y(both[2], 2) + from_y(both[1], 3)
    positive = summed[rank:, : count // 2].reshape(count)
    own = lax.dynamic_slice_in_dim(lse, me * count, count, 0)
    pos_loss = jnp.where(valid[:count], own - positive, 0.0)
    b_part = summed[:rank]
    for mask in (1, 2):
        b_part = b_part + plane_pair(b_part, mask)
    b_part = add_after(b_part, plane_pair(b_part, 4), [returned])
    b_grad = exchange(jnp.broadcast_to(b_part[None], (users, rank, share)), "user")
    b_grad = b_grad.transpose(1, 0, 2).reshape(rank, part_width)
    return (pos_loss, emb_grad, b_grad)


def solution(mesh):
    placed = (
        P(("item", "user"), "mp"),
        P("mp", None),
        P(None, "mp"),
        P("mp"),
        P(("item", "user"), "mp"),
        P(("item", "user"), None),
        P(("item", "user")),
    )
    return jax.shard_map(
        body,
        mesh=mesh,
        in_specs=placed,
        out_specs=(P(("item", "user")), P(("item", "user"), "mp"), P(None, "mp")),
        check_vma=False,
    )
```

```python
import math

import jax
import jax.numpy as jnp
from jax import lax
from jax.experimental import pallas as pl
from jax.experimental.pallas import tpu as pltpu
from jax.sharding import PartitionSpec as P

MODEL_WIDTH = 4096
LEN = 48
EPS = 1e-06
LOWEST = -1e30
MIB = 1024 * 1024


def exchange(x, axis):
    return lax.all_to_all(x, axis, split_axis=0, concat_axis=0, tiled=True)


def swap(x):
    return lax.ppermute(x, "mp", [(0, 1), (1, 0)])


def turn(x, by):
    return lax.dynamic_slice_in_dim(jnp.concatenate([x, x[:3]]), by, 4, 0)


def from_x(x, step):
    pairs = [((u // 4 + step) % 4 * 4 + u % 4, u) for u in range(16)]
    return lax.ppermute(x, "user", pairs)


def from_y(x, step):
    pairs = [(u // 4 * 4 + (u % 4 + step) % 4, u) for u in range(16)]
    return lax.ppermute(x, "user", pairs)


def add_kernel(left_ref, right_ref, *refs):
    refs[-1][...] = left_ref[...] + right_ref[...]


def add_after(left, right, pieces):
    vmem = pl.BlockSpec(memory_space=pltpu.VMEM)
    return pl.pallas_call(
        add_kernel,
        out_shape=jax.ShapeDtypeStruct(left.shape, left.dtype),
        in_specs=[vmem, vmem] + [pl.BlockSpec(memory_space=pl.ANY)] * len(pieces),
        out_specs=vmem,
        compiler_params=pltpu.CompilerParams(vmem_limit_bytes=4 * MIB),
        cost_estimate=pl.CostEstimate(
            flops=left.size, bytes_accessed=12 * left.size, transcendentals=0
        ),
    )(left, right, *pieces)


def plane_pair(x, mask):
    planes = lax.axis_size("item")
    return lax.ppermute(x, "item", [(z, z ^ mask) for z in range(planes)])


def body(
    item_last_hidden,
    frozen_down_weight,
    trained_up_weight,
    embedding_norm_gain,
    user_context_state,
    history_owner_device,
    history_item_row,
):
    stored, part_width = item_last_hidden.shape
    count = history_item_row.shape[0]
    planes = lax.axis_size("item")
    users = lax.axis_size("user")
    devices = planes * users
    group = users * count
    slots = 2 * users
    total = planes * slots
    me = lax.axis_index("user")

    queries = lax.all_gather(user_context_state, "user", axis=0, tiled=True)

    code = jnp.arange(count, dtype=jnp.int32) * stored + history_item_row
    named = history_owner_device == jnp.arange(devices, dtype=jnp.int32)[None, :]
    first = jnp.min(jnp.where(named, code[:, None], count * stored), axis=0)
    last = jnp.max(jnp.where(named, code[:, None], -1), axis=0)
    wanted = jnp.stack([jnp.where(last < 0, -1, first), jnp.where(last > first, last, -1)], axis=1)
    asked = exchange(wanted, ("item", "user")).reshape(planes, slots)
    asked = asked.reshape(total)
    my_x, my_y = me // 4, me % 4
    asked_row = jnp.where(asked < 0, -1 - my_x - my_y, asked % stored)
    asked_place = jnp.where(asked < 0, -1, asked // stored)

    rows = item_last_hidden[jnp.maximum(asked_row, 0)]
    note = jnp.broadcast_to(asked_place.astype(jnp.bfloat16)[:, None], (total, 128))
    packet = jnp.concatenate([rows, note], axis=1).reshape(planes, slots, part_width + 128)
    arrived = exchange(packet, "item").reshape(total, part_width + 128)
    hidden = arrived[:, :part_width]
    place = arrived[:, part_width].astype(jnp.int32)
    asker = (jnp.arange(total, dtype=jnp.int32) % slots) // 2
    used = place >= 0
    position = jnp.where(used, asker * count + place, -1)

    low = jnp.dot(hidden, frozen_down_weight, preferred_element_type=jnp.float32)
    low = low + swap(low)
    pre = hidden.astype(jnp.float32) + jnp.dot(
        low, trained_up_weight.astype(jnp.float32), precision=lax.Precision.HIGHEST
    )
    squares = jnp.sum(pre * pre, axis=1, keepdims=True)
    squares = squares + swap(squares)
    rinv = lax.rsqrt(squares / MODEL_WIDTH + EPS)
    hist = (pre * rinv * embedding_norm_gain).astype(jnp.bfloat16)

    line = jnp.arange(group, dtype=jnp.int32)
    valid = line % LEN != LEN - 1
    hit = (line[:, None] + 1 == position[None, :]) & valid[:, None]
    cut = group // 2
    partials = [
        lax.dot_general(
            part, hist, (((1,), (1,)), ((), ())), preferred_element_type=jnp.float32
        )
        for part in (queries[:cut], queries[cut:])
    ]
    sums = jnp.concatenate([partial + swap(partial) for partial in partials], axis=0)
    scores = jnp.where(used[None, :], sums / math.sqrt(MODEL_WIDTH), LOWEST)
    top = jnp.max(scores, axis=1)
    mass = jnp.sum(jnp.where(used[None, :], jnp.exp(scores - top[:, None]), 0.0), axis=1)
    positive = jnp.sum(jnp.where(hit, scores, 0.0), axis=1)
    stats = jnp.stack([top, mass])
    stats = exchange(jnp.broadcast_to(stats[None], (users, 2, group)), "user")
    peak = jnp.max(stats[:, 0], axis=0)
    lse = peak + jnp.log(jnp.sum(stats[:, 1] * jnp.exp(stats[:, 0] - peak[None]), axis=0))

    positive = jnp.where(lse > LOWEST, positive, 0.0)
    dscore = jnp.where(used[None, :], jnp.exp(scores - lse[:, None]), 0.0) - hit.astype(jnp.float32)
    dscore = jnp.where(valid[:, None], dscore, 0.0).astype(jnp.bfloat16)
    hist_grad = lax.dot_general(
        dscore, queries, (((0,), (0,)), ((), ())), preferred_element_type=jnp.float32
    ).astype(jnp.bfloat16)

    outgoing = hist_grad.reshape(planes, slots, part_width)
    returned = exchange(outgoing, "item").reshape(total, part_width)
    picker = (jnp.arange(stored, dtype=jnp.int32)[:, None] == asked_row[None, :]).astype(
        jnp.bfloat16
    )
    emb_grad = jnp.dot(picker, returned, preferred_element_type=jnp.float32)

    scaled = hist_grad.astype(jnp.float32) * embedding_norm_gain
    inner = jnp.sum(pre * scaled, axis=1, keepdims=True)
    inner = (inner + swap(inner)) / MODEL_WIDTH
    dpre = rinv * scaled - pre * rinv * rinv * rinv * inner
    b_part = jnp.dot(low.T, dpre, precision=lax.Precision.HIGHEST)
    rank = b_part.shape[0]
    share = part_width // users
    b_part = b_part.reshape(rank, users, share).transpose(1, 0, 2)
    positive = jnp.pad(positive.reshape(users, 2, count // 2), ((0, 0), (0, 0), (0, share - count // 2)))
    both = jnp.concatenate([b_part, positive], axis=1).reshape(4, 4, rank + 2, share)
    both = turn(both, my_x)
    both = both[0] + from_x(both[3], 1) + from_x(both[2], 2) + from_x(both[1], 3)
    both = (both + from_y(both, 2)) + (from_y(both, 1) + from_y(both, 3))
    summed = lax.dynamic_index_in_dim(both, my_y, 0, keepdims=False)
    positive = summed[rank:, : count // 2].reshape(count)
    own = lax.dynamic_slice_in_dim(lse, me * count, count, 0)
    pos_loss = jnp.where(valid[:count], own - positive, 0.0)
    b_part = both[:, :rank]
    for mask in (1, 2):
        b_part = b_part + plane_pair(b_part, mask)
    b_part = add_after(b_part, plane_pair(b_part, 4), [returned])
    b_grad = jnp.stack([b_part] + [from_x(b_part, step) for step in (1, 2, 3)])
    b_grad = turn(b_grad, (4 - my_x) % 4)
    b_grad = b_grad.transpose(2, 0, 1, 3).reshape(rank, part_width)
    return (pos_loss, emb_grad, b_grad)


def solution(mesh):
    placed = (
        P(("item", "user"), "mp"),
        P("mp", None),
        P(None, "mp"),
        P("mp"),
        P(("item", "user"), "mp"),
        P(("item", "user"), None),
        P(("item", "user")),
    )
    return jax.shard_map(
        body,
        mesh=mesh,
        in_specs=placed,
        out_specs=(P(("item", "user")), P(("item", "user"), "mp"), P(None, "mp")),
        check_vma=False,
    )
```

```python
import math

import jax
import jax.numpy as jnp
from jax import lax
from jax.experimental import pallas as pl
from jax.experimental.pallas import tpu as pltpu
from jax.sharding import PartitionSpec as P

MODEL_WIDTH = 4096
LEN = 48
EPS = 1e-06
LOWEST = -1e30
MIB = 1024 * 1024


def exchange(x, axis):
    return lax.all_to_all(x, axis, split_axis=0, concat_axis=0, tiled=True)


def swap(x):
    return lax.ppermute(x, "mp", [(0, 1), (1, 0)])


def turn(x, by):
    return lax.dynamic_slice_in_dim(jnp.concatenate([x, x[:3]]), by, 4, 0)


def from_x(x, step):
    pairs = [((u // 4 + step) % 4 * 4 + u % 4, u) for u in range(16)]
    return lax.ppermute(x, "user", pairs)


def from_y(x, step):
    pairs = [(u // 4 * 4 + (u % 4 + step) % 4, u) for u in range(16)]
    return lax.ppermute(x, "user", pairs)


def add_kernel(left_ref, right_ref, *refs):
    refs[-1][...] = left_ref[...] + right_ref[...]


def add_after(left, right, pieces):
    vmem = pl.BlockSpec(memory_space=pltpu.VMEM)
    return pl.pallas_call(
        add_kernel,
        out_shape=jax.ShapeDtypeStruct(left.shape, left.dtype),
        in_specs=[vmem, vmem] + [pl.BlockSpec(memory_space=pl.ANY)] * len(pieces),
        out_specs=vmem,
        compiler_params=pltpu.CompilerParams(vmem_limit_bytes=4 * MIB),
        cost_estimate=pl.CostEstimate(
            flops=left.size, bytes_accessed=12 * left.size, transcendentals=0
        ),
    )(left, right, *pieces)


def plane_pair(x, mask):
    planes = lax.axis_size("item")
    return lax.ppermute(x, "item", [(z, z ^ mask) for z in range(planes)])


def body(
    item_last_hidden,
    frozen_down_weight,
    trained_up_weight,
    embedding_norm_gain,
    user_context_state,
    history_owner_device,
    history_item_row,
):
    stored, part_width = item_last_hidden.shape
    count = history_item_row.shape[0]
    planes = lax.axis_size("item")
    users = lax.axis_size("user")
    devices = planes * users
    group = users * count
    slots = 2 * users
    total = planes * slots
    me = lax.axis_index("user")

    queries = lax.all_gather(user_context_state, "user", axis=0, tiled=True)

    code = jnp.arange(count, dtype=jnp.int32) * stored + history_item_row
    named = history_owner_device == jnp.arange(devices, dtype=jnp.int32)[None, :]
    first = jnp.min(jnp.where(named, code[:, None], count * stored), axis=0)
    last = jnp.max(jnp.where(named, code[:, None], -1), axis=0)
    wanted = jnp.stack([jnp.where(last < 0, -1, first), jnp.where(last > first, last, -1)], axis=1)
    asked = exchange(wanted, ("item", "user")).reshape(planes, slots)
    asked = asked.reshape(total)
    my_x, my_y = me // 4, me % 4
    asked_row = jnp.where(asked < 0, -1 - my_x - my_y, asked % stored)
    asked_place = jnp.where(asked < 0, -1, asked // stored)

    rows = item_last_hidden[jnp.maximum(asked_row, 0)]
    note = jnp.broadcast_to(asked_place.astype(jnp.bfloat16)[:, None], (total, 128))
    packet = jnp.concatenate([rows, note], axis=1).reshape(planes, slots, part_width + 128)
    arrived = exchange(packet, "item").reshape(total, part_width + 128)
    hidden = arrived[:, :part_width]
    place = arrived[:, part_width].astype(jnp.int32)
    asker = (jnp.arange(total, dtype=jnp.int32) % slots) // 2
    used = place >= 0
    position = jnp.where(used, asker * count + place, -1)

    low = jnp.dot(hidden, frozen_down_weight, preferred_element_type=jnp.float32)
    low = low + swap(low)
    pre = hidden.astype(jnp.float32) + jnp.dot(
        low, trained_up_weight.astype(jnp.float32), precision=lax.Precision.HIGHEST
    )
    squares = jnp.sum(pre * pre, axis=1, keepdims=True)
    squares = squares + swap(squares)
    rinv = lax.rsqrt(squares / MODEL_WIDTH + EPS)
    hist = (pre * rinv * embedding_norm_gain).astype(jnp.bfloat16)
    hist = lax.optimization_barrier(hist)

    line = jnp.arange(group, dtype=jnp.int32)
    valid = line % LEN != LEN - 1
    hit = (line[:, None] + 1 == position[None, :]) & valid[:, None]
    cut = group // 3 * 2
    partials = [
        lax.dot_general(
            part, hist, (((1,), (1,)), ((), ())), preferred_element_type=jnp.float32
        )
        for part in (queries[:cut], queries[cut:])
    ]
    sums = jnp.concatenate([partial + swap(partial) for partial in partials], axis=0)
    scores = jnp.where(used[None, :], sums / math.sqrt(MODEL_WIDTH), LOWEST)
    top = jnp.max(scores, axis=1)
    mass = jnp.sum(jnp.where(used[None, :], jnp.exp(scores - top[:, None]), 0.0), axis=1)
    positive = jnp.sum(jnp.where(hit, scores, 0.0), axis=1)
    stats = jnp.stack([top, mass])
    stats = exchange(jnp.broadcast_to(stats[None], (users, 2, group)), "user")
    peak = jnp.max(stats[:, 0], axis=0)
    lse = peak + jnp.log(jnp.sum(stats[:, 1] * jnp.exp(stats[:, 0] - peak[None]), axis=0))

    positive = jnp.where(lse > LOWEST, positive, 0.0)
    dscore = jnp.where(used[None, :], jnp.exp(scores - lse[:, None]), 0.0) - hit.astype(jnp.float32)
    dscore = jnp.where(valid[:, None], dscore, 0.0).astype(jnp.bfloat16)
    hist_grad = lax.dot_general(
        dscore, queries, (((0,), (0,)), ((), ())), preferred_element_type=jnp.float32
    ).astype(jnp.bfloat16)

    outgoing = hist_grad.reshape(planes, slots, part_width)
    returned = exchange(outgoing, "item").reshape(total, part_width)
    picker = (jnp.arange(stored, dtype=jnp.int32)[:, None] == asked_row[None, :]).astype(
        jnp.bfloat16
    )
    emb_grad = jnp.dot(picker, returned, preferred_element_type=jnp.float32)

    scaled = hist_grad.astype(jnp.float32) * embedding_norm_gain
    inner = jnp.sum(pre * scaled, axis=1, keepdims=True)
    inner = (inner + swap(inner)) / MODEL_WIDTH
    dpre = rinv * scaled - pre * rinv * rinv * rinv * inner
    b_part = jnp.dot(low.T, dpre, precision=lax.Precision.HIGH)
    rank = b_part.shape[0]
    share = part_width // users
    b_part = b_part.reshape(rank, users, share).transpose(1, 0, 2)
    positive = jnp.pad(positive.reshape(users, 2, count // 2), ((0, 0), (0, 0), (0, share - count // 2)))
    both = jnp.concatenate([b_part, positive], axis=1).reshape(4, 4, rank + 2, share)
    both = turn(both, my_x)
    both = both[0] + from_x(both[3], 1) + from_x(both[2], 2) + from_x(both[1], 3)
    both = (both + from_y(both, 2)) + (from_y(both, 1) + from_y(both, 3))
    summed = lax.dynamic_index_in_dim(both, my_y, 0, keepdims=False)
    positive = summed[rank:, : count // 2].reshape(count)
    own = lax.dynamic_slice_in_dim(lse, me * count, count, 0)
    pos_loss = jnp.where(valid[:count], own - positive, 0.0)
    b_part = both[:, :rank]
    b_part = (b_part + plane_pair(b_part, 1)) + (plane_pair(b_part, 2) + plane_pair(b_part, 3))
    b_part = add_after(b_part, plane_pair(b_part, 4), [returned])
    b_grad = jnp.stack([b_part] + [from_x(b_part, step) for step in (1, 2, 3)])
    b_grad = turn(b_grad, (4 - my_x) % 4)
    b_grad = b_grad.transpose(2, 0, 1, 3).reshape(rank, part_width)
    return (pos_loss, emb_grad, b_grad)


def solution(mesh):
    placed = (
        P(("item", "user"), "mp"),
        P("mp", None),
        P(None, "mp"),
        P("mp"),
        P(("item", "user"), "mp"),
        P(("item", "user"), None),
        P(("item", "user")),
    )
    return jax.shard_map(
        body,
        mesh=mesh,
        in_specs=placed,
        out_specs=(P(("item", "user")), P(("item", "user"), "mp"), P(None, "mp")),
        check_vma=False,
    )
```

```python
import math

import jax
import jax.numpy as jnp
from jax import lax
from jax.experimental import pallas as pl
from jax.experimental.pallas import tpu as pltpu
from jax.sharding import PartitionSpec as P

MODEL_WIDTH = 4096
LEN = 48
EPS = 1e-06
LOWEST = -1e30
MIB = 1024 * 1024


def exchange(x, axis):
    return lax.all_to_all(x, axis, split_axis=0, concat_axis=0, tiled=True)


def swap(x):
    return lax.ppermute(x, "mp", [(0, 1), (1, 0)])


def thirds_product(x, y):
    high = lax.reduce_precision(x, 8, 7)
    middle = lax.reduce_precision(x - high, 8, 7)
    parts = jnp.concatenate([high, middle, x - high - middle], axis=1).astype(jnp.bfloat16)
    product = lax.dot_general(
        parts, y, (((0,), (0,)), ((), ())), preferred_element_type=jnp.float32
    )
    return jnp.sum(product.reshape(3, x.shape[1], y.shape[1]), axis=0)


def turn(x, by):
    return lax.dynamic_slice_in_dim(jnp.concatenate([x, x[:3]]), by, 4, 0)


def from_x(x, step):
    pairs = [((u // 4 + step) % 4 * 4 + u % 4, u) for u in range(16)]
    return lax.ppermute(x, "user", pairs)


def from_y(x, step):
    pairs = [(u // 4 * 4 + (u % 4 + step) % 4, u) for u in range(16)]
    return lax.ppermute(x, "user", pairs)


def add_kernel(left_ref, right_ref, *refs):
    refs[-1][...] = left_ref[...] + right_ref[...]


def add_after(left, right, pieces):
    vmem = pl.BlockSpec(memory_space=pltpu.VMEM)
    return pl.pallas_call(
        add_kernel,
        out_shape=jax.ShapeDtypeStruct(left.shape, left.dtype),
        in_specs=[vmem, vmem] + [pl.BlockSpec(memory_space=pl.ANY)] * len(pieces),
        out_specs=vmem,
        compiler_params=pltpu.CompilerParams(vmem_limit_bytes=4 * MIB),
        cost_estimate=pl.CostEstimate(
            flops=left.size, bytes_accessed=12 * left.size, transcendentals=0
        ),
    )(left, right, *pieces)


def plane_pair(x, mask):
    planes = lax.axis_size("item")
    return lax.ppermute(x, "item", [(z, z ^ mask) for z in range(planes)])


def body(
    item_last_hidden,
    frozen_down_weight,
    trained_up_weight,
    embedding_norm_gain,
    user_context_state,
    history_owner_device,
    history_item_row,
):
    stored, part_width = item_last_hidden.shape
    count = history_item_row.shape[0]
    planes = lax.axis_size("item")
    users = lax.axis_size("user")
    devices = planes * users
    group = users * count
    slots = 2 * users
    total = planes * slots
    me = lax.axis_index("user")

    queries = lax.all_gather(user_context_state, "user", axis=0, tiled=True)

    code = jnp.arange(count, dtype=jnp.int32) * stored + history_item_row
    named = history_owner_device == jnp.arange(devices, dtype=jnp.int32)[None, :]
    first = jnp.min(jnp.where(named, code[:, None], count * stored), axis=0)
    last = jnp.max(jnp.where(named, code[:, None], -1), axis=0)
    wanted = jnp.stack([jnp.where(last < 0, -1, first), jnp.where(last > first, last, -1)], axis=1)
    asked = exchange(wanted, ("item", "user")).reshape(planes, slots)
    asked = asked.reshape(total)
    my_x, my_y = me // 4, me % 4
    asked_row = jnp.where(asked < 0, -1 - my_x - my_y, asked % stored)
    asked_place = jnp.where(asked < 0, -1, asked // stored)

    rows = item_last_hidden[jnp.maximum(asked_row, 0)]
    note = jnp.broadcast_to(asked_place.astype(jnp.bfloat16)[:, None], (total, 128))
    packet = jnp.concatenate([rows, note], axis=1).reshape(planes, slots, part_width + 128)
    arrived = exchange(packet, "item").reshape(total, part_width + 128)
    hidden = arrived[:, :part_width]
    place = arrived[:, part_width].astype(jnp.int32)
    asker = (jnp.arange(total, dtype=jnp.int32) % slots) // 2
    used = place >= 0
    position = jnp.where(used, asker * count + place, -1)

    low = jnp.dot(hidden, frozen_down_weight, preferred_element_type=jnp.float32)
    low = low + swap(low)
    pre = hidden.astype(jnp.float32) + jnp.dot(
        low, trained_up_weight.astype(jnp.float32), precision=lax.Precision.HIGHEST
    )
    squares = jnp.sum(pre * pre, axis=1, keepdims=True)
    squares = squares + swap(squares)
    rinv = lax.rsqrt(squares / MODEL_WIDTH + EPS)
    hist = (pre * rinv * embedding_norm_gain).astype(jnp.bfloat16)
    hist = lax.optimization_barrier(hist)

    line = jnp.arange(group, dtype=jnp.int32)
    valid = line % LEN != LEN - 1
    hit = (line[:, None] + 1 == position[None, :]) & valid[:, None]
    cut = group // 3 * 2
    partials = [
        lax.dot_general(
            part, hist, (((1,), (1,)), ((), ())), preferred_element_type=jnp.float32
        )
        for part in (queries[:cut], queries[cut:])
    ]
    sums = jnp.concatenate([partial + swap(partial) for partial in partials], axis=0)
    scores = jnp.where(used[None, :], sums / math.sqrt(MODEL_WIDTH), LOWEST)
    top = jnp.max(scores, axis=1)
    mass = jnp.sum(jnp.where(used[None, :], jnp.exp(scores - top[:, None]), 0.0), axis=1)
    positive = jnp.sum(jnp.where(hit, scores, 0.0), axis=1)
    stats = jnp.stack([top, mass])
    stats = exchange(jnp.broadcast_to(stats[None], (users, 2, group)), "user")
    peak = jnp.max(stats[:, 0], axis=0)
    lse = peak + jnp.log(jnp.sum(stats[:, 1] * jnp.exp(stats[:, 0] - peak[None]), axis=0))

    positive = jnp.where(lse > LOWEST, positive, 0.0)
    dscore = jnp.where(used[None, :], jnp.exp(scores - lse[:, None]), 0.0) - hit.astype(jnp.float32)
    dscore = jnp.where(valid[:, None], dscore, 0.0).astype(jnp.bfloat16)
    hist_grad = lax.dot_general(
        dscore, queries, (((0,), (0,)), ((), ())), preferred_element_type=jnp.float32
    ).astype(jnp.bfloat16)

    outgoing = hist_grad.reshape(planes, slots, part_width)
    returned = exchange(outgoing, "item").reshape(total, part_width)
    picker = (jnp.arange(stored, dtype=jnp.int32)[:, None] == asked_row[None, :]).astype(
        jnp.bfloat16
    )
    emb_grad = jnp.dot(picker, returned, preferred_element_type=jnp.float32)

    scaled = hist_grad.astype(jnp.float32) * embedding_norm_gain
    inner = jnp.sum(pre * scaled, axis=1, keepdims=True)
    inner = (inner + swap(inner)) / MODEL_WIDTH
    bend = low * (rinv * rinv * rinv * inner)
    b_part = thirds_product(low * rinv, hist_grad) * embedding_norm_gain
    b_part = b_part - thirds_product(bend, hidden)
    b_part = b_part - jnp.dot(
        jnp.dot(bend.T, low, precision=lax.Precision.HIGHEST),
        trained_up_weight.astype(jnp.float32),
        precision=lax.Precision.HIGHEST,
    )
    rank = b_part.shape[0]
    share = part_width // users
    b_part = b_part.reshape(rank, users, share).transpose(1, 0, 2)
    positive = jnp.pad(positive.reshape(users, 2, count // 2), ((0, 0), (0, 0), (0, share - count // 2)))
    both = jnp.concatenate([b_part, positive], axis=1).reshape(4, 4, rank + 2, share)
    both = turn(both, my_x)
    both = both[0] + from_x(both[3], 1) + from_x(both[2], 2) + from_x(both[1], 3)
    both = (both + from_y(both, 2)) + (from_y(both, 1) + from_y(both, 3))
    summed = lax.dynamic_index_in_dim(both, my_y, 0, keepdims=False)
    positive = summed[rank:, : count // 2].reshape(count)
    own = lax.dynamic_slice_in_dim(lse, me * count, count, 0)
    pos_loss = jnp.where(valid[:count], own - positive, 0.0)
    b_part = both[:, :rank]
    b_part = (b_part + plane_pair(b_part, 1)) + (plane_pair(b_part, 2) + plane_pair(b_part, 3))
    b_part = add_after(b_part, plane_pair(b_part, 4), [returned])
    b_grad = jnp.stack([b_part] + [from_x(b_part, step) for step in (1, 2, 3)])
    b_grad = turn(b_grad, (4 - my_x) % 4)
    b_grad = b_grad.transpose(2, 0, 1, 3).reshape(rank, part_width)
    return (pos_loss, emb_grad, b_grad)


def solution(mesh):
    placed = (
        P(("item", "user"), "mp"),
        P("mp", None),
        P(None, "mp"),
        P("mp"),
        P(("item", "user"), "mp"),
        P(("item", "user"), None),
        P(("item", "user")),
    )
    return jax.shard_map(
        body,
        mesh=mesh,
        in_specs=placed,
        out_specs=(P(("item", "user")), P(("item", "user"), "mp"), P(None, "mp")),
        check_vma=False,
    )
```
